512 devices in a mesh: band: 16 (over z_lo, core), tile: 32 (over x, z_hi, y).
Axes of the slice: x: 4, y: 4, z: 16 (z_hi: 2, z_lo: 8; z = z_hi * 8 + z_lo), core: 2. Of those that a mesh axis runs over, the one named last changes fastest.
Arguments:
- raw_traces: bfloat16 [32, 4096, 2048], P('tile', 'band'), may hold values from -6 to 6
- bin_owner: int32 [32, 4096, 1], P('tile'), may hold values from 0 to 31; in each aligned block of 4096 rows (0 to 4095, 4096 to 8191, ..., all dimensions but the last counted through in order) at most 256 rows name the same one
- bin_offset: int32 [32, 4096], P('tile'), may hold values from 0 to 8191
Outputs:
- multiples: float32 [160, 2, 512, 512], P('band', None, 'tile')
The draws below stay inside these ranges and needn't reach their ends.
Inputs may be any that keep to these rules, and one draw needn't show every extreme that they name: `bin_owner`: in each tile's list of 4096 traces at most 256 are binned into one tile, and some tile receives exactly 256.
All inputs are finite; a program needn't handle non-finite values.
Results may differ from the reference program's by a relative error of at most 0.0067.
Values may be sent and summed in bfloat16 or wider, within the bound.
A program may use at most 128 MiB of HBM per device.

```python
import math
import jax
import jax.numpy as jnp
import numpy as np
from jax import lax

NG = 512
NT = 2048
FB = 10
NF = 160
TILES = 32
TR_TILE = 4096
CAP = 256
CELLS_DEV = 8192
N_BAND = 16
N_TILE = 32


def plant(entries, own_key, low, high):
    longest = entries.shape.index(max(entries.shape))
    spots = []
    for shift in (0, 1):
        where = [jax.random.randint(jax.random.fold_in(own_key, axis), (), 0, length) for axis, length in enumerate(entries.shape)]
        where[longest] = (where[longest] + shift) % entries.shape[longest]
        spots.append(tuple(where))
    return entries.at[spots[0]].set(low).at[spots[1]].set(high)


def level_of(key, extent, cuts, least, top_value):
    def one(position, parts):
        heights = jax.random.uniform(jax.random.fold_in(jax.random.fold_in(key, 6), position), (parts,), jnp.float32, least / len(cuts), top_value / len(cuts))
        return jnp.repeat(jnp.exp(heights), extent[position] // parts).reshape((-1,) + (1,) * (len(extent) - position - 1))

    level = one(*cuts[0])
    for cut in cuts[1:]:
        level = level * one(*cut)
    return level


def shared_out(key, own, number, rows, count, top, reach, skew):
    ranking = jax.random.permutation(key, count)
    crowded, usual = shares(count, rows * top, reach, skew, True), shares(count, rows * top, reach, skew, False)
    places = jnp.arange(count)

    def named(lengths, turn):
        used = int((lengths > 0).sum())
        fixed = max(1, used // 4)
        passed = fixed + (places - fixed + turn * (used - fixed)) % max(1, count - fixed)
        return jnp.zeros((count,), jnp.int32).at[ranking[jnp.where(places < fixed, places, passed)]].set(jnp.asarray(lengths, jnp.int32))

    lengths = jnp.where(number % 4 == 0, named(crowded, number // 4), named(usual, number - number // 4 - 1))
    mixed = jax.random.permutation(jax.random.fold_in(own, 3), count)
    source_of, taker = mixed[0:count // 2 * 2:2], mixed[1:count // 2 * 2:2]
    margin = jnp.minimum(lengths[source_of] - 1, reach - lengths[taker]) // 2
    margin = jnp.where((source_of == ranking[0]) | (taker == ranking[0]) | (lengths[taker] == 0), 0, jnp.maximum(margin, 0))
    passed = jax.random.randint(jax.random.fold_in(own, 4), (count // 2,), 0, 1 << 20) % (margin + 1)
    lengths = lengths.at[source_of].add(-passed).at[taker].add(passed)
    members = jnp.searchsorted(jnp.cumsum(lengths), jnp.arange(rows * top), side="right").astype(jnp.int32)
    grid = members.reshape(top, rows).T
    grid = grid[jax.random.permutation(jax.random.fold_in(own, 1), rows)]
    turn = jax.random.randint(jax.random.fold_in(own, 2), (rows, 1), 0, top)
    return jnp.take_along_axis(grid, (jnp.arange(top)[None, :] + turn) % top, axis=1)


def shares(amount, total, limit, slope, full):
    weights = [(1 << 20) // math.isqrt(standing ** slope) + 1 for standing in range(1, amount + 1)]
    largest = limit if full else min(limit, max(-(-total // amount), total * weights[0] // sum(weights)))
    least = 1 if total - largest >= amount - 1 else 0
    given, rest = [largest] + [least] * (amount - 1), total - largest - least * (amount - 1)
    while rest > 0:
        movable = [i for i in range(1, amount) if given[i] < largest] or [i for i in range(1, amount) if given[i] < limit]
        whole, remaining = sum([weights[i] for i in movable]), rest
        for i in movable:
            more = min(limit - given[i], max(1, remaining * weights[i] // whole), rest)
            given[i] = given[i] + more
            rest = rest - more
    return np.array(given)


def centred(stream_key, shape, scale, most, split=(), kind=jnp.bfloat16):
    level = level_of(stream_key, shape, split, -0.22, 0.18) if split else 1.0
    result = jax.random.normal(stream_key, shape, jnp.float32) * scale * level
    return jnp.minimum(jnp.maximum(result, -most), most).astype(kind)


def setup_inputs(seed: int = 0) -> dict:
    splits = jax.random.split(jax.random.key(seed), 4)
    raw_traces = centred(splits[0], (TILES, TR_TILE, NT), 1.0, 6.0, ((0, 32), (1, 16)))
    bin_owner_keys = jax.random.split(jax.random.fold_in(splits[1], 1), TILES * TR_TILE // TR_TILE)
    bin_owner_turns = jax.random.permutation(jax.random.fold_in(splits[1], 3), TILES * TR_TILE // TR_TILE)
    bin_owner = jax.vmap(lambda own, number: shared_out(jax.random.fold_in(splits[1], 2), own, number, TR_TILE, N_TILE, 1, CAP, 2))(bin_owner_keys, bin_owner_turns).reshape((TILES, TR_TILE, 1))
    bin_offset = plant(jax.random.randint(splits[2], (TILES, TR_TILE), 0, CELLS_DEV), jax.random.fold_in(splits[2], 1), 0, CELLS_DEV - 1).astype(jnp.int32)
    return {"raw_traces": raw_traces, "bin_owner": bin_owner, "bin_offset": bin_offset}


def twiddle_band(first_freq, freq_count):
    time_index = jnp.arange(NT, dtype=jnp.int32)
    freq_index = jnp.arange(freq_count, dtype=jnp.int32) + first_freq + 1
    phase_angle = (time_index[:, None] * freq_index[None, :] % NT).astype(jnp.float32) * (2.0 * math.pi / NT)
    norm_factor = 1.0 / math.sqrt(NT)
    return jnp.concatenate([jnp.cos(phase_angle) * norm_factor, -jnp.sin(phase_angle) * norm_factor], axis=1).astype(jnp.bfloat16)

def reference(raw_traces, bin_owner, bin_offset):
    traces = raw_traces.reshape(TILES * TR_TILE, NT)
    cell_index = (bin_owner[:, :, 0] * CELLS_DEV + bin_offset).reshape(-1).astype(jnp.int32)
    counts = jax.ops.segment_sum(jnp.ones(cell_index.shape, jnp.float32), cell_index, NG * NG)
    divisor = jnp.maximum(counts, 1.0)
    out_scale = 1.0 / math.sqrt(NG)

    def per_band(band_index):
        twiddle = twiddle_band(band_index * FB, FB)
        spectra = jnp.dot(traces, twiddle, preferred_element_type=jnp.float32).astype(jnp.bfloat16)
        cell_sums = jax.ops.segment_sum(spectra.astype(jnp.float32), cell_index, NG * NG)
        grid_field = (cell_sums / divisor[:, None]).astype(jnp.bfloat16)
        grid_field = grid_field.T.reshape(2, FB, NG, NG).transpose(1, 0, 2, 3)
        wide = grid_field.astype(jnp.float32)
        symmetric = (0.5 * (wide + jnp.swapaxes(wide, 2, 3))).astype(jnp.bfloat16)
        real_part = symmetric[:, 0].astype(jnp.float32)
        imag_part = symmetric[:, 1].astype(jnp.float32)
        product_real = jnp.einsum('fik,fkj->fij', real_part, real_part) - jnp.einsum('fik,fkj->fij', imag_part, imag_part)
        product_imag = jnp.einsum('fik,fkj->fij', real_part, imag_part) + jnp.einsum('fik,fkj->fij', imag_part, real_part)
        return jnp.stack([product_real, product_imag], axis=1) * out_scale
    stacked = lax.map(per_band, jnp.arange(N_BAND, dtype=jnp.int32))
    return stacked.reshape(NF, 2, NG, NG)
```

```python
import math

import jax
import jax.numpy as jnp
import numpy as np
from jax import lax
from jax.experimental import pallas as pl
from jax.experimental.pallas import tpu as pltpu
from jax.sharding import PartitionSpec as P

NG = 512
NT = 2048
FB = 10
NB = 16
NTILE = 32
HF = 5
ROWS = 16
CH = 256
MESH = pl.DeviceIdType.MESH
F32 = jnp.float32
BF16 = jnp.bfloat16


def twiddle_rows():
    time = np.arange(NT, dtype=np.int64)
    table = np.zeros((2, NB, ROWS, NT), np.float64)
    for half in range(2):
        for band in range(NB):
            for i in range(HF):
                k = band * FB + half * HF + i + 1
                angle = 2.0 * math.pi * ((time * k) % NT) / NT
                table[half, band, 2 * i] = np.cos(angle) / math.sqrt(NT)
                table[half, band, 2 * i + 1] = -np.sin(angle) / math.sqrt(NT)
    return table.reshape(2 * NB * ROWS, NT).astype(np.float32).astype(jnp.bfloat16)


def tile_of(chip, half):
    return (chip // 4) * 8 + half * 4 + chip % 4


def shift_of(z):
    return (z * 5) % 16


def handler_chip(n, z):
    n0 = (n + 16 - shift_of(z)) % 16
    x = n0 % 4
    y = (n0 // 4 + x) % 4
    return x * 4 + y


def handler_number(chip, z):
    x = chip // 4
    y = chip % 4
    return (4 * ((y + 4 - x) % 4) + x + shift_of(z)) % 16


def onehot_groups(chunks, key_row, lo_row, l_ref, r_ref):
    low = lax.broadcasted_iota(jnp.int32, (CH, CH), 0).astype(F32).astype(BF16)
    zero = jnp.zeros((ROWS, CH), BF16)
    for n, chunk in enumerate(chunks):
        wide = chunk.astype(F32)
        key = jnp.broadcast_to(wide[key_row : key_row + 1], (ROWS, CH)).astype(BF16)
        lo = jnp.broadcast_to(wide[lo_row : lo_row + 1], (ROWS, CH)).astype(BF16)
        cols = slice(n * CH, (n + 1) * CH)
        for k in range(32):
            l_ref[k * ROWS : (k + 1) * ROWS, cols] = jnp.where(key == BF16(k), chunk, zero)
        lo_all = jnp.concatenate([lo] * (CH // ROWS), axis=0)
        r_ref[:, cols] = jnp.where(low == lo_all, BF16(1), BF16(0))


def nt_dot(left, right):
    return lax.dot_general(left, right, (((1,), (1,)), ((), ())), preferred_element_type=F32)


def kernel(
    raw_ref, tw_ref, own_ref, off_ref, out_ref,
    send1, rc1, l_ref, r_ref, acc_ref, send2, rc2, g_ref, rc3, s1, s2, mout,
    sem1s, sem1r, sem2s, sem2r, sem3s, sem3r, sem4s, sem4r,
):
    band = lax.axis_index("band")
    tile = lax.axis_index("tile")
    x = tile // 8
    half = (tile // 4) % 2
    y = tile % 4
    chip = x * 4 + y
    zlo = band // 2
    core = band % 2
    z = half * 8 + zlo
    me1 = half * NB + band

    def at_column(d):
        return {"band": d % NB, "tile": x * 8 + (d // NB) * 4 + y}

    def at_plane(c, h):
        return {"band": band, "tile": tile_of(c, h)}

    barrier = pltpu.get_barrier_semaphore()

    def greet_column(r, carry):
        d = (me1 + r) % 32
        pl.semaphore_signal(barrier, inc=1, device_id=at_column(d), device_id_type=MESH)
        return carry

    def greet_plane(r, carry):
        c = (chip + r) % 16
        pl.semaphore_signal(barrier, inc=1, device_id=at_plane(c, half), device_id_type=MESH)
        pl.semaphore_signal(barrier, inc=1, device_id=at_plane(c, 1 - half), device_id_type=MESH)
        return carry

    lax.fori_loop(1, 32, greet_column, 0)
    lax.fori_loop(1, 16, greet_plane, 0)

    ids = lax.broadcasted_iota(jnp.int32, (32, 128), 0)

    def owner_code(t):
        return (t // 8) * 8 + (t % 4) * 2 + (t // 4) % 2

    def count(i, carry):
        row = jnp.broadcast_to(owner_code(own_ref[pl.ds(i, 1), :]), (32, 128))
        before = jnp.where(i < 2 * band, 1.0, 0.0)
        return carry + jnp.where(row == ids, 1.0, 0.0) * before

    counts = lax.fori_loop(0, 32, count, jnp.zeros((32, 128), F32))
    counts = jnp.sum(counts, axis=1, keepdims=True)
    own = jnp.concatenate([own_ref[pl.ds(2 * band, 1), :], own_ref[pl.ds(2 * band + 1, 1), :]], axis=1)
    off = jnp.concatenate([off_ref[pl.ds(2 * band, 1), :], off_ref[pl.ds(2 * band + 1, 1), :]], axis=1)
    own = owner_code(own)
    hits = jnp.broadcast_to(own, (32, CH)) == lax.broadcasted_iota(jnp.int32, (32, CH), 0)
    hits = jnp.where(hits, 1.0, 0.0)
    earlier = lax.broadcasted_iota(jnp.int32, (CH, CH), 0) < lax.broadcasted_iota(jnp.int32, (CH, CH), 1)
    earlier = jnp.where(earlier, 1.0, 0.0).astype(BF16)
    ahead = jnp.dot(hits.astype(BF16), earlier, preferred_element_type=F32)
    rank = jnp.sum(hits * (ahead + counts), axis=0, keepdims=True)
    column = off % NG
    key2 = (column // CH) * 16 + off // NG
    row_id = lax.broadcasted_iota(jnp.int32, (ROWS, CH), 0)
    labels = jnp.where(row_id == 10, 1.0, 0.0)
    for at, value in ((11, own.astype(F32)), (12, rank), (13, key2.astype(F32)), (14, (column % CH).astype(F32))):
        labels = labels + jnp.where(row_id == at, jnp.broadcast_to(value, (ROWS, CH)), 0.0)

    spectra = nt_dot(tw_ref[...], raw_ref[...]).reshape(2 * NB, ROWS, CH)
    send1[...] = (spectra + labels[None]).astype(BF16)

    pl.semaphore_wait(barrier, 31 + 30)

    def copy1(d):
        return pltpu.make_async_remote_copy(
            src_ref=send1.at[d], dst_ref=rc1.at[me1], send_sem=sem1s.at[d], recv_sem=sem1r.at[me1],
            device_id=at_column(d), device_id_type=MESH,
        )

    def start1(r, carry):
        copy1((me1 + r) % 32).start()
        return carry

    own1 = pltpu.make_async_copy(send1.at[me1], rc1.at[me1], sem1r.at[me1])
    own1.start()
    lax.fori_loop(1, 32, start1, 0)

    for lst in range(2):
        def slot(g, carry):
            for n in range(4):
                src = lst * NB + g * 4 + n
                pltpu.make_async_copy(rc1.at[src], rc1.at[src], sem1r.at[src]).wait()
            onehot_groups([rc1[lst * NB + g * 4 + n] for n in range(4)], 11, 12, l_ref, r_ref)
            part = nt_dot(l_ref[...], r_ref[...])
            acc_ref[0] += part
            return carry

        acc_ref[0] = jnp.zeros((512, CH), F32)
        lax.fori_loop(0, 4, slot, 0)
        send2[:, :, lst] = acc_ref[0].reshape(16, 2, ROWS, CH).astype(BF16)

    def copy2(c):
        return pltpu.make_async_remote_copy(
            src_ref=send2.at[c], dst_ref=rc2.at[chip], send_sem=sem2s.at[c], recv_sem=sem2r.at[chip],
            device_id=at_plane(c, half), device_id_type=MESH,
        )

    def start2(r, carry):
        copy2((chip + r) % 16).start()
        return carry

    own2 = pltpu.make_async_copy(send2.at[chip], rc2.at[chip], sem2r.at[chip])
    own2.start()
    lax.fori_loop(1, 16, start2, 0)

    def bin_group(g, carry):
        for n in range(2):
            src = g * 2 + n
            pltpu.make_async_copy(rc2.at[src], rc2.at[src], sem2r.at[src]).wait()
        for h in range(2):
            chunks = [rc2[g * 2 + n // 2, h, n % 2] for n in range(4)]
            onehot_groups(chunks, 13, 14, l_ref, r_ref)
            part = nt_dot(l_ref[...], r_ref[...])
            acc_ref[h] += part
        return carry

    acc_ref[...] = jnp.zeros_like(acc_ref)
    lax.fori_loop(0, 8, bin_group, 0)
    for h in range(2):
        for hi in range(2):
            block = acc_ref[h, hi * 256 : (hi + 1) * 256].reshape(16, ROWS, CH)
            block = block / jnp.maximum(block[:, 10:11, :], 1.0)
            block = jnp.swapaxes(block, 0, 1).astype(BF16)
            for v in range(2 * HF):
                g_ref[v // 2, v % 2, h, :, hi * CH : (hi + 1) * CH] = block[v]

    def copy3(i, h):
        c = handler_chip(core * HF + i, z)
        rows = pl.ds(pl.multiple_of(16 * tile_of(chip, h), 16), 16)
        remote = pltpu.make_async_remote_copy(
            src_ref=g_ref.at[i, :, h], dst_ref=rc3.at[:, rows], send_sem=sem3s.at[i, h], recv_sem=sem3r,
            device_id=at_plane(c, half), device_id_type=MESH,
        )
        local = pltpu.make_async_copy(g_ref.at[i, :, h], rc3.at[:, rows], sem3r)
        return c, remote, local

    for i in range(HF):
        for h in range(2):
            c, remote, local = copy3(i, h)

            @pl.when(c != chip)
            def _():
                remote.start()

            @pl.when(c == chip)
            def _():
                local.start()

    number = handler_number(chip, z) - core * HF
    place = half * HF + number

    def copy4(t):
        h = (t // 4) % 2
        c = (t // 8) * 4 + t % 4
        return pltpu.make_async_remote_copy(
            src_ref=mout.at[t], dst_ref=out_ref.at[place], send_sem=sem4s.at[t], recv_sem=sem4r,
            device_id=at_plane(c, h), device_id_type=MESH,
        )

    own4 = pltpu.make_async_copy(mout.at[tile], out_ref.at[place], sem4r)

    @pl.when((number >= 0) & (number < HF))
    def _():
        pltpu.make_async_copy(rc3, rc3, sem3r).wait()
        for p in range(2):
            wide = rc3[p].astype(F32)
            sym = (0.5 * (wide + wide.T)).astype(BF16)
            s1[p * NG : (p + 1) * NG, :] = sym
            s2[(1 - p) * NG : (2 - p) * NG, :] = sym

        def rows(b, carry):
            at = pl.ds(pl.multiple_of(b * 256, 256), 256)
            at_imag = pl.ds(pl.multiple_of(NG + b * 256, 256), 256)
            real, imag = s1[at, :], s1[at_imag, :]
            m_real = jnp.dot(jnp.concatenate([real, -imag], axis=1), s1[...], preferred_element_type=F32)
            m_imag = jnp.dot(jnp.concatenate([real, imag], axis=1), s2[...], preferred_element_type=F32)
            scale = 1.0 / math.sqrt(NG)
            mout[pl.ds(b * 16, 16), 0] = (m_real * scale).astype(BF16).reshape(16, 16, NG)
            mout[pl.ds(b * 16, 16), 1] = (m_imag * scale).astype(BF16).reshape(16, 16, NG)

            def send(u, carry):
                t = b * 16 + u

                @pl.when(t != tile)
                def _():
                    copy4(t).start()

                @pl.when(t == tile)
                def _():
                    own4.start()

                return carry

            return lax.fori_loop(0, 16, send, carry)

        lax.fori_loop(0, 2, rows, 0)

        def sent(t, carry):
            @pl.when(t != tile)
            def _():
                copy4(t).wait_send()

            return carry

        lax.fori_loop(0, 32, sent, 0)

    def sent1(r, carry):
        copy1((me1 + r) % 32).wait_send()
        return carry

    def sent2(r, carry):
        copy2((chip + r) % 16).wait_send()
        return carry

    lax.fori_loop(1, 32, sent1, 0)
    lax.fori_loop(1, 16, sent2, 0)
    for i in range(HF):
        for h in range(2):
            c, remote, local = copy3(i, h)

            @pl.when(c != chip)
            def _():
                remote.wait_send()

    pltpu.make_async_copy(out_ref, out_ref, sem4r).wait()


def per_device(raw_traces, bin_owner, bin_offset, twiddle):
    vmem = pl.BlockSpec(memory_space=pltpu.VMEM)
    strips = pl.pallas_call(
        kernel,
        out_shape=jax.ShapeDtypeStruct((FB, 2, 16, NG), BF16),
        in_specs=[vmem] * 4,
        out_specs=vmem,
        scratch_shapes=[
            pltpu.VMEM((32, ROWS, CH), BF16),
            pltpu.VMEM((32, ROWS, CH), BF16),
            pltpu.VMEM((512, 4 * CH), BF16),
            pltpu.VMEM((CH, 4 * CH), BF16),
            pltpu.VMEM((2, 512, CH), F32),
            pltpu.VMEM((16, 2, 2, ROWS, CH), BF16),
            pltpu.VMEM((16, 2, 2, ROWS, CH), BF16),
            pltpu.VMEM((HF, 2, 2, 16, NG), BF16),
            pltpu.VMEM((2, NG, NG), BF16),
            pltpu.VMEM((2 * NG, NG), BF16),
            pltpu.VMEM((2 * NG, NG), BF16),
            pltpu.VMEM((NTILE, 2, 16, NG), BF16),
            pltpu.SemaphoreType.DMA((32,)),
            pltpu.SemaphoreType.DMA((32,)),
            pltpu.SemaphoreType.DMA((16,)),
            pltpu.SemaphoreType.DMA((16,)),
            pltpu.SemaphoreType.DMA((HF, 2)),
            pltpu.SemaphoreType.DMA,
            pltpu.SemaphoreType.DMA((32,)),
            pltpu.SemaphoreType.DMA,
        ],
        compiler_params=pltpu.CompilerParams(
            collective_id=0, has_side_effects=True, vmem_limit_bytes=40 * 1024 * 1024
        ),
    )(
        raw_traces.reshape(CH, NT),
        twiddle,
        bin_owner.reshape(32, 128),
        bin_offset.reshape(32, 128),
    )
    return strips.astype(F32)


def solution(mesh):
    table = twiddle_rows()
    step = jax.shard_map(
        per_device,
        mesh=mesh,
        in_specs=(P("tile", "band", None), P("tile", None, None), P("tile", None), P(None, None)),
        out_specs=P("band", None, "tile", None),
        check_vma=False,
    )
    return lambda raw_traces, bin_owner, bin_offset: step(raw_traces, bin_owner, bin_offset, jnp.asarray(table))
```

```python
import math

import jax
import jax.numpy as jnp
import numpy as np
from jax import lax
from jax.experimental import pallas as pl
from jax.experimental.pallas import tpu as pltpu
from jax.sharding import PartitionSpec as P

NG = 512
NT = 2048
FB = 10
NB = 16
NTILE = 32
HF = 5
ROWS = 16
CH = 256
MESH = pl.DeviceIdType.MESH
F32 = jnp.float32
BF16 = jnp.bfloat16


def twiddle_rows():
    time = np.arange(NT, dtype=np.int64)
    table = np.zeros((2, NB, ROWS, NT), np.float64)
    for half in range(2):
        for band in range(NB):
            for i in range(HF):
                k = band * FB + half * HF + i + 1
                angle = 2.0 * math.pi * ((time * k) % NT) / NT
                table[half, band, 2 * i] = np.cos(angle) / math.sqrt(NT)
                table[half, band, 2 * i + 1] = -np.sin(angle) / math.sqrt(NT)
    table = np.roll(table.reshape(2 * NB, ROWS, NT), 8, axis=0)
    return table.reshape(2 * NB * ROWS, NT).astype(np.float32).astype(jnp.bfloat16)


def tile_of(chip, half):
    return (chip // 4) * 8 + half * 4 + chip % 4


def shift_of(z):
    return (z * 5) % 16


def handler_chip(n, z):
    n0 = (n + 16 - shift_of(z)) % 16
    x = n0 % 4
    y = (n0 // 4 + x) % 4
    return x * 4 + y


def handler_number(chip, z):
    x = chip // 4
    y = chip % 4
    return (4 * ((y + 4 - x) % 4) + x + shift_of(z)) % 16


def onehot_groups(chunks, key_row, lo_row, l_ref, r_ref):
    low = lax.broadcasted_iota(jnp.int32, (CH, CH), 0).astype(F32).astype(BF16)
    zero = jnp.zeros((ROWS, CH), BF16)
    for n, chunk in enumerate(chunks):
        wide = chunk.astype(F32)
        key = jnp.broadcast_to(wide[key_row : key_row + 1], (ROWS, CH)).astype(BF16)
        lo = jnp.broadcast_to(wide[lo_row : lo_row + 1], (ROWS, CH)).astype(BF16)
        cols = slice(n * CH, (n + 1) * CH)
        for k in range(32):
            l_ref[k * ROWS : (k + 1) * ROWS, cols] = jnp.where(key == BF16(k), chunk, zero)
        lo_all = jnp.concatenate([lo] * (CH // ROWS), axis=0)
        r_ref[:, cols] = jnp.where(low == lo_all, BF16(1), BF16(0))


def onehot_cells(chunks, l_ref, r_ref):
    low = lax.broadcasted_iota(jnp.int32, (CH, CH), 0).astype(F32).astype(BF16)
    keys = lax.broadcasted_iota(jnp.int32, (32, CH), 0).astype(F32).astype(BF16)
    zero = jnp.zeros((32, CH), BF16)
    for n, chunk in enumerate(chunks):
        wide = chunk.astype(F32)

        def spread(row, rows):
            tile = jnp.broadcast_to(wide[row : row + 1], (ROWS, CH)).astype(BF16)
            return jnp.concatenate([tile] * (rows // ROWS), axis=0)

        cols = slice(n * CH, (n + 1) * CH)
        mask = spread(13, 32) == keys
        for v in range(11):
            l_ref[v * 32 : (v + 1) * 32, cols] = jnp.where(mask, spread(v, 32), zero)
        r_ref[:, cols] = jnp.where(low == spread(14, CH), BF16(1), BF16(0))


def nt_dot(left, right):
    return lax.dot_general(left, right, (((1,), (1,)), ((), ())), preferred_element_type=F32)


def kernel(
    raw_hbm, tw_hbm, own_hbm, off_hbm, out_ref,
    raw_ref, tw_ref, own_ref, off_ref,
    send1, rc1, l_ref, r_ref, acc_ref, send2, rc2, g_ref, rc3, s1, s2, mout,
    sem_in, sem1s, sem1r, sem2s, sem2r, sem3s, sem3r, sem4s, sem4r,
):
    band = lax.axis_index("band")
    tile = lax.axis_index("tile")
    x = tile // 8
    half = (tile // 4) % 2
    y = tile % 4
    chip = x * 4 + y
    zlo = band // 2
    core = band % 2
    z = half * 8 + zlo
    me1 = half * NB + band
    part = ((z + 12) % 16) // 8
    home = ((z + 12) % 8) * 2 + core

    def at_column(d):
        return {"band": d % NB, "tile": x * 8 + (d // NB) * 4 + y}

    def at_plane(c):
        return {"band": band, "tile": tile_of(c, half)}

    def at_level(c, level):
        return {"band": (level % 8) * 2 + core, "tile": tile_of(c, level // 8)}

    def column(r):
        return ((half + r // NB) % 2) * NB + (band + r) % NB

    barrier = pltpu.get_barrier_semaphore()

    def greet_column(r, carry):
        pl.semaphore_signal(barrier, inc=1, device_id=at_column(column(r)), device_id_type=MESH)
        return carry

    def greet_plane(r, carry):
        c = (chip + r) % 16
        pl.semaphore_signal(barrier, inc=1, device_id=at_plane(c), device_id_type=MESH)
        pl.semaphore_signal(barrier, inc=1, device_id=at_level(c, (z + 4) % 16), device_id_type=MESH)
        pl.semaphore_signal(barrier, inc=1, device_id=at_level(c, (z + 12) % 16), device_id_type=MESH)
        return carry

    loads = [
        pltpu.make_async_copy(src, dst, sem_in.at[n])
        for n, (src, dst) in enumerate(
            ((own_hbm, own_ref), (off_hbm, off_ref), (raw_hbm, raw_ref), (tw_hbm, tw_ref))
        )
    ]
    for load in loads:
        load.start()
    lax.fori_loop(1, 32, greet_column, 0)
    lax.fori_loop(1, 16, greet_plane, 0)

    loads[0].wait()
    loads[1].wait()
    ids = lax.broadcasted_iota(jnp.int32, (32, 128), 0)

    def owner_code(t):
        return (t // 8) * 8 + (t % 4) * 2 + (t // 4) % 2

    def count(i, carry):
        row = jnp.broadcast_to(owner_code(own_ref[pl.ds(i, 1), :]), (32, 128))
        before = jnp.where(i < 2 * band, 1.0, 0.0)
        return carry + jnp.where(row == ids, 1.0, 0.0) * before

    counts = lax.fori_loop(0, 32, count, jnp.zeros((32, 128), F32))
    counts = jnp.sum(counts, axis=1, keepdims=True)
    own = jnp.concatenate([own_ref[pl.ds(2 * band, 1), :], own_ref[pl.ds(2 * band + 1, 1), :]], axis=1)
    off = jnp.concatenate([off_ref[pl.ds(2 * band, 1), :], off_ref[pl.ds(2 * band + 1, 1), :]], axis=1)
    own = owner_code(own)
    hits = jnp.broadcast_to(own, (32, CH)) == lax.broadcasted_iota(jnp.int32, (32, CH), 0)
    hits = jnp.where(hits, 1.0, 0.0)
    earlier = lax.broadcasted_iota(jnp.int32, (CH, CH), 0) < lax.broadcasted_iota(jnp.int32, (CH, CH), 1)
    earlier = jnp.where(earlier, 1.0, 0.0).astype(BF16)
    ahead = jnp.dot(hits.astype(BF16), earlier, preferred_element_type=F32)
    rank = jnp.sum(hits * (ahead + counts), axis=0, keepdims=True)
    place = off % NG
    key2 = (place // CH) * 16 + off // NG
    row_id = lax.broadcasted_iota(jnp.int32, (ROWS, CH), 0)
    labels = jnp.where(row_id == 10, 1.0, 0.0)
    for at, value in ((11, own.astype(F32)), (12, rank), (13, key2.astype(F32)), (14, (place % CH).astype(F32))):
        labels = labels + jnp.where(row_id == at, jnp.broadcast_to(value, (ROWS, CH)), 0.0)

    loads[2].wait()
    loads[3].wait()
    spectra = nt_dot(tw_ref[...], raw_ref[...]).reshape(2 * NB, ROWS, CH)
    send1[...] = (spectra + labels[None]).astype(BF16)

    pl.semaphore_wait(barrier, 31 + 45)

    def copy1(d):
        return pltpu.make_async_remote_copy(
            src_ref=send1.at[d], dst_ref=rc1.at[me1], send_sem=sem1s.at[d], recv_sem=sem1r.at[me1],
            device_id=at_column(d), device_id_type=MESH,
        )

    def start1(r, carry):
        copy1(column(r)).start()
        return carry

    own1 = pltpu.make_async_copy(send1.at[me1], rc1.at[me1], sem1r.at[me1])
    own1.start()
    lax.fori_loop(1, 32, start1, 0)

    def copy2(s, c):
        return pltpu.make_async_remote_copy(
            src_ref=send2.at[s, c], dst_ref=rc2.at[s, chip], send_sem=sem2s.at[s, c], recv_sem=sem2r.at[s, chip],
            device_id=at_plane(c), device_id_type=MESH,
        )

    for s in range(2):
        first = ((half + s) % 2) * NB

        def slot(g, carry):
            sources = []
            for n in range(2):
                k = (1 - s) * 7 + (2 * s - 1) * (g * 2 + n)
                k = (zlo + 12 + ((k + 1) // 2) * (1 - 2 * (k % 2))) % 8
                sources += [first + 2 * k, first + 2 * k + 1]
            for src in sources:
                pltpu.make_async_copy(rc1.at[src], rc1.at[src], sem1r.at[src]).wait()
            onehot_groups([rc1[src] for src in sources], 11, 12, l_ref, r_ref)
            acc_ref[0] += nt_dot(l_ref[...], r_ref[...])
            return carry

        def start2(r, carry):
            copy2(s, (chip + r) % 16).start()
            return carry

        acc_ref[0] = jnp.zeros((512, CH), F32)
        lax.fori_loop(0, 4, slot, 0)
        send2[s] = acc_ref[0].reshape(16, 2, ROWS, CH).astype(BF16)
        own2 = pltpu.make_async_copy(send2.at[s, chip], rc2.at[s, chip], sem2r.at[s, chip])
        own2.start()
        lax.fori_loop(1, 16, start2, 0)

    def copy3(i, h):
        c = handler_chip(core * HF + i, z)
        rows = pl.ds(pl.multiple_of(16 * tile_of(chip, h), 16), 16)
        remote = pltpu.make_async_remote_copy(
            src_ref=g_ref.at[i, :, h], dst_ref=rc3.at[:, rows], send_sem=sem3s.at[i, h], recv_sem=sem3r,
            device_id=at_plane(c), device_id_type=MESH,
        )
        local = pltpu.make_async_copy(g_ref.at[i, :, h], rc3.at[:, rows], sem3r)
        return c, remote, local

    acc_ref[...] = jnp.zeros_like(acc_ref)
    for s in range(2):
        def bin_group(g, carry):
            sources = [(chip + g * 4 + n) % 16 for n in range(4)]
            for src in sources:
                pltpu.make_async_copy(rc2.at[s, src], rc2.at[s, src], sem2r.at[s, src]).wait()
            for h in range(2):
                onehot_cells([rc2[s, src, h] for src in sources], l_ref, r_ref)
                acc_ref[h, :352] += nt_dot(l_ref[:352], r_ref[...])
            return carry

        lax.fori_loop(0, 4, bin_group, 0)

    for h in range(2):
        for hi in range(2):
            many = acc_ref[h, 320 + hi * 16 : 336 + hi * 16, :]
            share = 1.0 / jnp.maximum(many, 1.0)
            for v in range(2 * HF):
                mean = acc_ref[h, v * 32 + hi * 16 : v * 32 + hi * 16 + 16, :] * share
                g_ref[v // 2, v % 2, h, :, hi * CH : (hi + 1) * CH] = mean.astype(BF16)
        for i in range(HF):
            c, remote, local = copy3(i, h)

            @pl.when(c != chip)
            def _():
                remote.start()

            @pl.when(c == chip)
            def _():
                local.start()

    number = handler_number(chip, z) - core * HF
    place4 = part * HF + number

    def copy4(t):
        return pltpu.make_async_remote_copy(
            src_ref=mout.at[t], dst_ref=out_ref.at[place4], send_sem=sem4s.at[t], recv_sem=sem4r,
            device_id={"band": home, "tile": t}, device_id_type=MESH,
        )

    @pl.when((number >= 0) & (number < HF))
    def _():
        pltpu.make_async_copy(rc3, rc3, sem3r).wait()
        for p in range(2):
            wide = rc3[p].astype(F32)
            sym = (0.5 * (wide + wide.T)).astype(BF16)
            s1[p * NG : (p + 1) * NG, :] = sym
            s2[(1 - p) * NG : (2 - p) * NG, :] = sym

        def rows(b, carry):
            at = pl.ds(pl.multiple_of(b * 256, 256), 256)
            at_imag = pl.ds(pl.multiple_of(NG + b * 256, 256), 256)
            real, imag = s1[at, :], s1[at_imag, :]
            m_real = jnp.dot(jnp.concatenate([real, -imag], axis=1), s1[...], preferred_element_type=F32)
            m_imag = jnp.dot(jnp.concatenate([real, imag], axis=1), s2[...], preferred_element_type=F32)
            scale = 1.0 / math.sqrt(NG)
            mout[pl.ds(b * 16, 16), 0] = (m_real * scale).astype(BF16).reshape(16, 16, NG)
            mout[pl.ds(b * 16, 16), 1] = (m_imag * scale).astype(BF16).reshape(16, 16, NG)

            def send(u, carry):
                copy4(tile_of(b * 8 + (chip + u // 2) % 8, u % 2)).start()
                return carry

            return lax.fori_loop(0, 16, send, carry)

        lax.fori_loop(0, 2, rows, 0)

        def sent(t, carry):
            copy4(t).wait_send()
            return carry

        lax.fori_loop(0, 32, sent, 0)

    def sent1(r, carry):
        copy1(column(r)).wait_send()
        return carry

    def sent2(r, carry):
        copy2(0, (chip + r) % 16).wait_send()
        copy2(1, (chip + r) % 16).wait_send()
        return carry

    lax.fori_loop(1, 32, sent1, 0)
    lax.fori_loop(1, 16, sent2, 0)
    for i in range(HF):
        for h in range(2):
            c, remote, local = copy3(i, h)

            @pl.when(c != chip)
            def _():
                remote.wait_send()

    pltpu.make_async_copy(out_ref, out_ref, sem4r).wait()


def per_device(raw_traces, bin_owner, bin_offset, twiddle):
    vmem = pl.BlockSpec(memory_space=pltpu.VMEM)
    anywhere = pl.BlockSpec(memory_space=pltpu.HBM)
    strips = pl.pallas_call(
        kernel,
        out_shape=jax.ShapeDtypeStruct((FB, 2, 16, NG), BF16),
        in_specs=[anywhere] * 4,
        out_specs=vmem,
        scratch_shapes=[
            pltpu.VMEM((CH, NT), BF16),
            pltpu.VMEM((2 * NB * ROWS, NT), BF16),
            pltpu.VMEM((32, 128), jnp.int32),
            pltpu.VMEM((32, 128), jnp.int32),
            pltpu.VMEM((32, ROWS, CH), BF16),
            pltpu.VMEM((32, ROWS, CH), BF16),
            pltpu.VMEM((512, 4 * CH), BF16),
            pltpu.VMEM((CH, 4 * CH), BF16),
            pltpu.VMEM((2, 512, CH), F32),
            pltpu.VMEM((2, 16, 2, ROWS, CH), BF16),
            pltpu.VMEM((2, 16, 2, ROWS, CH), BF16),
            pltpu.VMEM((HF, 2, 2, 16, NG), BF16),
            pltpu.VMEM((2, NG, NG), BF16),
            pltpu.VMEM((2 * NG, NG), BF16),
            pltpu.VMEM((2 * NG, NG), BF16),
            pltpu.VMEM((NTILE, 2, 16, NG), BF16),
            pltpu.SemaphoreType.DMA((4,)),
            pltpu.SemaphoreType.DMA((32,)),
            pltpu.SemaphoreType.DMA((32,)),
            pltpu.SemaphoreType.DMA((2, 16)),
            pltpu.SemaphoreType.DMA((2, 16)),
            pltpu.SemaphoreType.DMA((HF, 2)),
            pltpu.SemaphoreType.DMA,
            pltpu.SemaphoreType.DMA((32,)),
            pltpu.SemaphoreType.DMA,
        ],
        compiler_params=pltpu.CompilerParams(
            collective_id=0, has_side_effects=True, vmem_limit_bytes=60 * 1024 * 1024
        ),
    )(
        raw_traces.reshape(CH, NT),
        twiddle,
        bin_owner.reshape(32, 128),
        bin_offset.reshape(32, 128),
    )
    return strips.astype(F32)


def solution(mesh):
    table = twiddle_rows()
    step = jax.shard_map(
        per_device,
        mesh=mesh,
        in_specs=(P("tile", "band", None), P("tile", None, None), P("tile", None), P(None, None)),
        out_specs=P("band", None, "tile", None),
        check_vma=False,
    )
    return lambda raw_traces, bin_owner, bin_offset: step(raw_traces, bin_owner, bin_offset, jnp.asarray(table))
```

```python
import math

import jax
import jax.numpy as jnp
import numpy as np
from jax import lax
from jax.experimental import pallas as pl
from jax.experimental.pallas import tpu as pltpu
from jax.sharding import PartitionSpec as P

NG = 512
NT = 2048
FB = 10
NB = 16
NTILE = 32
HF = 5
ROWS = 16
CH = 256
MESH = pl.DeviceIdType.MESH
F32 = jnp.float32
BF16 = jnp.bfloat16


def twiddle_rows():
    time = np.arange(NT, dtype=np.int64)
    table = np.zeros((2, NB, ROWS, NT), np.float64)
    for half in range(2):
        for band in range(NB):
            for i in range(HF):
                k = band * FB + half * HF + i + 1
                angle = 2.0 * math.pi * ((time * k) % NT) / NT
                table[half, band, 2 * i] = np.cos(angle) / math.sqrt(NT)
                table[half, band, 2 * i + 1] = -np.sin(angle) / math.sqrt(NT)
    table = np.roll(table.reshape(2 * NB, ROWS, NT), 8, axis=0)
    return table.reshape(2 * NB * ROWS, NT).astype(np.float32).astype(jnp.bfloat16)


def tile_of(chip, half):
    return (chip // 4) * 8 + half * 4 + chip % 4


def shift_of(z):
    return (z * 4) % 16


def handler_chip(n, z):
    n0 = (n + 16 - shift_of(z)) % 16
    x = n0 % 4
    y = (n0 // 4 + x) % 4
    return x * 4 + y


def handler_number(chip, z):
    x = chip // 4
    y = chip % 4
    return (4 * ((y + 4 - x) % 4) + x + shift_of(z)) % 16


def onehot_groups(chunks, key_row, lo_row, l_ref, r_ref):
    low = lax.broadcasted_iota(jnp.int32, (CH, CH), 0).astype(F32).astype(BF16)
    zero = jnp.zeros((ROWS, CH), BF16)
    for n, chunk in enumerate(chunks):
        wide = chunk.astype(F32)
        key = jnp.broadcast_to(wide[key_row : key_row + 1], (ROWS, CH)).astype(BF16)
        lo = jnp.broadcast_to(wide[lo_row : lo_row + 1], (ROWS, CH)).astype(BF16)
        cols = slice(n * CH, (n + 1) * CH)
        for k in range(32):
            l_ref[k * ROWS : (k + 1) * ROWS, cols] = jnp.where(key == BF16(k), chunk, zero)
        lo_all = jnp.concatenate([lo] * (CH // ROWS), axis=0)
        r_ref[:, cols] = jnp.where(low == lo_all, BF16(1), BF16(0))


def onehot_cells(chunks, l_ref, r_ref):
    low = lax.broadcasted_iota(jnp.int32, (CH, CH), 0).astype(F32).astype(BF16)
    keys = lax.broadcasted_iota(jnp.int32, (32, CH), 0).astype(F32).astype(BF16)
    zero = jnp.zeros((32, CH), BF16)
    for n, chunk in enumerate(chunks):
        wide = chunk.astype(F32)

        def spread(row, rows):
            tile = jnp.broadcast_to(wide[row : row + 1], (ROWS, CH)).astype(BF16)
            return jnp.concatenate([tile] * (rows // ROWS), axis=0)

        cols = slice(n * CH, (n + 1) * CH)
        mask = spread(13, 32) == keys
        for v in range(11):
            l_ref[v * 32 : (v + 1) * 32, cols] = jnp.where(mask, spread(v, 32), zero)
        r_ref[:, cols] = jnp.where(low == spread(14, CH), BF16(1), BF16(0))


def nt_dot(left, right):
    return lax.dot_general(left, right, (((1,), (1,)), ((), ())), preferred_element_type=F32)


def kernel(
    raw_hbm, tw_hbm, own_hbm, off_hbm, out_ref,
    raw_ref, tw_ref, own_ref, off_ref,
    send1, rc1, l_ref, r_ref, acc_ref, send2, rc2, g_ref, rc3, s1, s2, mout,
    sem_in, sem1s, sem1r, sem2s, sem2r, sem3s, sem3r, sem4s, sem4r,
):
    band = lax.axis_index("band")
    tile = lax.axis_index("tile")
    x = tile // 8
    half = (tile // 4) % 2
    y = tile % 4
    chip = x * 4 + y
    zlo = band // 2
    core = band % 2
    z = half * 8 + zlo
    me1 = half * NB + band
    part = ((z + 12) % 16) // 8
    home = ((z + 12) % 8) * 2 + core

    def at_column(d):
        return {"band": d % NB, "tile": x * 8 + (d // NB) * 4 + y}

    def at_plane(c):
        return {"band": band, "tile": tile_of(c, half)}

    def at_level(c, level):
        return {"band": (level % 8) * 2 + core, "tile": tile_of(c, level // 8)}

    def column(r):
        return ((half + r // NB) % 2) * NB + (band + r) % NB

    barrier = pltpu.get_barrier_semaphore()

    def greet_column(r, carry):
        pl.semaphore_signal(barrier, inc=1, device_id=at_column(column(r)), device_id_type=MESH)
        return carry

    def greet_plane(r, carry):
        c = (chip + r) % 16
        pl.semaphore_signal(barrier, inc=1, device_id=at_plane(c), device_id_type=MESH)
        pl.semaphore_signal(barrier, inc=1, device_id=at_level(c, (z + 4) % 16), device_id_type=MESH)
        pl.semaphore_signal(barrier, inc=1, device_id=at_level(c, (z + 12) % 16), device_id_type=MESH)
        return carry

    loads = [
        pltpu.make_async_copy(src, dst, sem_in.at[n])
        for n, (src, dst) in enumerate(
            ((own_hbm, own_ref), (off_hbm, off_ref), (raw_hbm, raw_ref), (tw_hbm, tw_ref))
        )
    ]
    for load in loads:
        load.start()
    lax.fori_loop(1, 32, greet_column, 0)
    lax.fori_loop(1, 16, greet_plane, 0)

    loads[0].wait()
    loads[1].wait()
    ids = lax.broadcasted_iota(jnp.int32, (32, 128), 0)

    def owner_code(t):
        return (t // 8) * 8 + (t % 4) * 2 + (t // 4) % 2

    def count(i, carry):
        row = jnp.broadcast_to(owner_code(own_ref[pl.ds(i, 1), :]), (32, 128))
        before = jnp.where(i < 2 * band, 1.0, 0.0)
        return carry + jnp.where(row == ids, 1.0, 0.0) * before

    counts = lax.fori_loop(0, 32, count, jnp.zeros((32, 128), F32))
    counts = jnp.sum(counts, axis=1, keepdims=True)
    own = jnp.concatenate([own_ref[pl.ds(2 * band, 1), :], own_ref[pl.ds(2 * band + 1, 1), :]], axis=1)
    off = jnp.concatenate([off_ref[pl.ds(2 * band, 1), :], off_ref[pl.ds(2 * band + 1, 1), :]], axis=1)
    own = owner_code(own)
    hits = jnp.broadcast_to(own, (32, CH)) == lax.broadcasted_iota(jnp.int32, (32, CH), 0)
    hits = jnp.where(hits, 1.0, 0.0)
    earlier = lax.broadcasted_iota(jnp.int32, (CH, CH), 0) < lax.broadcasted_iota(jnp.int32, (CH, CH), 1)
    earlier = jnp.where(earlier, 1.0, 0.0).astype(BF16)
    ahead = jnp.dot(hits.astype(BF16), earlier, preferred_element_type=F32)
    rank = jnp.sum(hits * (ahead + counts), axis=0, keepdims=True)
    place = off % NG
    key2 = (place // CH) * 16 + off // NG
    row_id = lax.broadcasted_iota(jnp.int32, (ROWS, CH), 0)
    labels = jnp.where(row_id == 10, 1.0, 0.0)
    for at, value in ((11, own.astype(F32)), (12, rank), (13, key2.astype(F32)), (14, (place % CH).astype(F32))):
        labels = labels + jnp.where(row_id == at, jnp.broadcast_to(value, (ROWS, CH)), 0.0)

    loads[2].wait()
    loads[3].wait()
    spectra = nt_dot(tw_ref[...], raw_ref[...]).reshape(2 * NB, ROWS, CH)
    send1[...] = (spectra + labels[None]).astype(BF16)

    pl.semaphore_wait(barrier, 31 + 45)

    def copy1(d):
        return pltpu.make_async_remote_copy(
            src_ref=send1.at[d], dst_ref=rc1.at[me1], send_sem=sem1s.at[d], recv_sem=sem1r.at[me1],
            device_id=at_column(d), device_id_type=MESH,
        )

    def start1(r, carry):
        d = (((half + (r // 8) % 2) % 2) * 8 + (zlo + r % 8) % 8) * 2 + r // 16

        @pl.when(d != me1)
        def _():
            copy1(d).start()

        return carry

    own1 = pltpu.make_async_copy(send1.at[me1], rc1.at[me1], sem1r.at[me1])
    own1.start()
    lax.fori_loop(0, 32, start1, 0)

    def copy2(s, c):
        return pltpu.make_async_remote_copy(
            src_ref=send2.at[s, c], dst_ref=rc2.at[s, chip], send_sem=sem2s.at[s, c], recv_sem=sem2r.at[s, chip],
            device_id=at_plane(c), device_id_type=MESH,
        )

    for s in range(2):
        first = ((half + s) % 2) * NB

        def slot(g, carry):
            sources = []
            for n in range(2):
                k = (1 - s) * 7 + (2 * s - 1) * (g * 2 + n)
                k = (zlo + 12 + ((k + 1) // 2) * (1 - 2 * (k % 2))) % 8
                sources += [first + 2 * k, first + 2 * k + 1]
            for src in sources:
                pltpu.make_async_copy(rc1.at[src], rc1.at[src], sem1r.at[src]).wait()
            onehot_groups([rc1[src] for src in sources], 11, 12, l_ref, r_ref)
            acc_ref[0] += nt_dot(l_ref[...], r_ref[...])
            return carry

        def start2(r, carry):
            q = r % 4
            dx = (2 + 4 - r // 4 + (r // 8) * (7 - 2 * (r // 4))) % 4
            dy = (2 + 4 - q + (q // 2) * (7 - 2 * q)) % 4
            copy2(s, ((x + dx) % 4) * 4 + (y + dy) % 4).start()
            return carry

        acc_ref[0] = jnp.zeros((512, CH), F32)
        lax.fori_loop(0, 4, slot, 0)
        send2[s] = acc_ref[0].reshape(16, 2, ROWS, CH).astype(BF16)
        own2 = pltpu.make_async_copy(send2.at[s, chip], rc2.at[s, chip], sem2r.at[s, chip])
        own2.start()
        lax.fori_loop(0, 15, start2, 0)

    def copy3(i, h):
        rows = pl.ds(pl.multiple_of(16 * tile_of(chip, h), 16), 16)
        if i < 4:
            freq, level, c = i, z, handler_chip(core * 4 + i, z)
        else:
            level = (z + 4 + 8 * (i - 4)) % 16
            freq, c = 4, handler_chip(8 + core * 2 + i - 4, level)
        remote = pltpu.make_async_remote_copy(
            src_ref=g_ref.at[freq, :, h], dst_ref=rc3.at[:, rows], send_sem=sem3s.at[i, h], recv_sem=sem3r,
            device_id=at_level(c, level), device_id_type=MESH,
        )
        local = pltpu.make_async_copy(g_ref.at[freq, :, h], rc3.at[:, rows], sem3r)
        return (c == chip) & (level == z), remote, local

    acc_ref[...] = jnp.zeros_like(acc_ref)
    for s in range(2):
        def bin_group(g, carry):
            sources = [(chip + g * 4 + n) % 16 for n in range(4)]
            for src in sources:
                pltpu.make_async_copy(rc2.at[s, src], rc2.at[s, src], sem2r.at[s, src]).wait()
            for h in range(2):
                onehot_cells([rc2[s, src, h] for src in sources], l_ref, r_ref)
                acc_ref[h, :352] += nt_dot(l_ref[:352], r_ref[...])
            return carry

        lax.fori_loop(0, 4, bin_group, 0)

    for h in range(2):
        for hi in range(2):
            many = acc_ref[h, 320 + hi * 16 : 336 + hi * 16, :]
            share = 1.0 / jnp.maximum(many, 1.0)
            for v in range(2 * HF):
                mean = acc_ref[h, v * 32 + hi * 16 : v * 32 + hi * 16 + 16, :] * share
                g_ref[v // 2, v % 2, h, :, hi * CH : (hi + 1) * CH] = mean.astype(BF16)
        for i in (4, 5, 0, 1, 2, 3):
            here, remote, local = copy3(i, h)
            if i >= 4:
                remote.start()
                continue

            @pl.when(jnp.logical_not(here))
            def _():
                remote.start()

            @pl.when(here)
            def _():
                local.start()

    number = handler_number(chip, z)
    far = number - core * 4
    near = number - 8 - core * 2
    is_far = (far >= 0) & (far < 4)
    is_near = (near >= 0) & (near < 2)
    far_place = part * HF + far
    near_place = ((half + 1 + near) % 2) * HF + 4

    def product(real, imag):
        m_real = jnp.dot(jnp.concatenate([real, -imag], axis=1), s1[...], preferred_element_type=F32)
        m_imag = jnp.dot(jnp.concatenate([real, imag], axis=1), s2[...], preferred_element_type=F32)
        scale = 1.0 / math.sqrt(NG)
        return [(m * scale).astype(BF16).reshape(16, 16, NG) for m in (m_real, m_imag)]

    def copy4(t):
        return pltpu.make_async_remote_copy(
            src_ref=mout.at[t], dst_ref=out_ref.at[far_place], send_sem=sem4s.at[t], recv_sem=sem4r,
            device_id={"band": home, "tile": t}, device_id_type=MESH,
        )

    def copy5(c):
        return pltpu.make_async_remote_copy(
            src_ref=mout.at[c], dst_ref=out_ref.at[near_place], send_sem=sem4s.at[c], recv_sem=sem4r,
            device_id=at_plane(c), device_id_type=MESH,
        )

    own5 = pltpu.make_async_copy(mout.at[chip], out_ref.at[near_place], sem4r)

    @pl.when(is_far | is_near)
    def _():
        pltpu.make_async_copy(rc3, rc3, sem3r).wait()
        for p in range(2):
            wide = rc3[p].astype(F32)
            sym = (0.5 * (wide + wide.T)).astype(BF16)
            s1[p * NG : (p + 1) * NG, :] = sym
            s2[(1 - p) * NG : (2 - p) * NG, :] = sym

    @pl.when(is_far)
    def _():
        def rows(turn, carry):
            b = (x // 2 + 1 + turn) % 2
            at = pl.ds(pl.multiple_of(b * 256, 256), 256)
            at_imag = pl.ds(pl.multiple_of(NG + b * 256, 256), 256)
            for p, m in enumerate(product(s1[at, :], s1[at_imag, :])):
                mout[pl.ds(b * 16, 16), p] = m

            def send(u, carry):
                q = u // 4
                up = (y + 2 + 4 - q + (q // 2) * (7 - 2 * q)) % 4
                along = 2 * b + (x + 1 + (u // 2) % 2) % 2
                copy4(tile_of(along * 4 + up, u % 2)).start()
                return carry

            return lax.fori_loop(0, 16, send, carry)

        lax.fori_loop(0, 2, rows, 0)

        def sent(t, carry):
            copy4(t).wait_send()
            return carry

        lax.fori_loop(0, 32, sent, 0)

    @pl.when(is_near)
    def _():
        real = [s1[pl.ds(pl.multiple_of(128 * n + 64 * half, 64), 64), :] for n in range(4)]
        imag = [s1[pl.ds(pl.multiple_of(NG + 128 * n + 64 * half, 64), 64), :] for n in range(4)]
        for p, m in enumerate(product(jnp.concatenate(real, axis=0), jnp.concatenate(imag, axis=0))):
            mout[:16, p] = m
        own5.start()

        def send(r, carry):
            copy5((chip + r) % 16).start()
            return carry

        def sent(r, carry):
            copy5((chip + r) % 16).wait_send()
            return carry

        lax.fori_loop(1, 16, send, 0)
        lax.fori_loop(1, 16, sent, 0)

    def sent1(r, carry):
        copy1(column(r)).wait_send()
        return carry

    def sent2(r, carry):
        copy2(0, (chip + r) % 16).wait_send()
        copy2(1, (chip + r) % 16).wait_send()
        return carry

    lax.fori_loop(1, 32, sent1, 0)
    lax.fori_loop(1, 16, sent2, 0)
    for i in range(6):
        for h in range(2):
            here, remote, local = copy3(i, h)
            if i >= 4:
                remote.wait_send()
                continue

            @pl.when(jnp.logical_not(here))
            def _():
                remote.wait_send()

    pltpu.make_async_copy(out_ref, out_ref, sem4r).wait()


def per_device(raw_traces, bin_owner, bin_offset, twiddle):
    vmem = pl.BlockSpec(memory_space=pltpu.VMEM)
    anywhere = pl.BlockSpec(memory_space=pltpu.HBM)
    strips = pl.pallas_call(
        kernel,
        out_shape=jax.ShapeDtypeStruct((FB, 2, 16, NG), BF16),
        in_specs=[anywhere] * 4,
        out_specs=vmem,
        scratch_shapes=[
            pltpu.VMEM((CH, NT), BF16),
            pltpu.VMEM((2 * NB * ROWS, NT), BF16),
            pltpu.VMEM((32, 128), jnp.int32),
            pltpu.VMEM((32, 128), jnp.int32),
            pltpu.VMEM((32, ROWS, CH), BF16),
            pltpu.VMEM((32, ROWS, CH), BF16),
            pltpu.VMEM((512, 4 * CH), BF16),
            pltpu.VMEM((CH, 4 * CH), BF16),
            pltpu.VMEM((2, 512, CH), F32),
            pltpu.VMEM((2, 16, 2, ROWS, CH), BF16),
            pltpu.VMEM((2, 16, 2, ROWS, CH), BF16),
            pltpu.VMEM((HF, 2, 2, 16, NG), BF16),
            pltpu.VMEM((2, NG, NG), BF16),
            pltpu.VMEM((2 * NG, NG), BF16),
            pltpu.VMEM((2 * NG, NG), BF16),
            pltpu.VMEM((NTILE, 2, 16, NG), BF16),
            pltpu.SemaphoreType.DMA((4,)),
            pltpu.SemaphoreType.DMA((32,)),
            pltpu.SemaphoreType.DMA((32,)),
            pltpu.SemaphoreType.DMA((2, 16)),
            pltpu.SemaphoreType.DMA((2, 16)),
            pltpu.SemaphoreType.DMA((6, 2)),
            pltpu.SemaphoreType.DMA,
            pltpu.SemaphoreType.DMA((32,)),
            pltpu.SemaphoreType.DMA,
        ],
        compiler_params=pltpu.CompilerParams(
            collective_id=0, has_side_effects=True, vmem_limit_bytes=60 * 1024 * 1024
        ),
    )(
        raw_traces.reshape(CH, NT),
        twiddle,
        bin_owner.reshape(32, 128),
        bin_offset.reshape(32, 128),
    )
    return strips.astype(F32)


def solution(mesh):
    table = twiddle_rows()
    step = jax.shard_map(
        per_device,
        mesh=mesh,
        in_specs=(P("tile", "band", None), P("tile", None, None), P("tile", None), P(None, None)),
        out_specs=P("band", None, "tile", None),
        check_vma=False,
    )
    return lambda raw_traces, bin_owner, bin_offset: step(raw_traces, bin_owner, bin_offset, jnp.asarray(table))
```

```python
import math

import jax
import jax.numpy as jnp
import numpy as np
from jax import lax
from jax.experimental import pallas as pl
from jax.experimental.pallas import tpu as pltpu
from jax.sharding import PartitionSpec as P

NG = 512
NT = 2048
FB = 10
NB = 16
NTILE = 32
HF = 5
ROWS = 16
CH = 256
MESH = pl.DeviceIdType.MESH
F32 = jnp.float32
BF16 = jnp.bfloat16


def twiddle_rows():
    time = np.arange(NT, dtype=np.int64)
    table = np.zeros((2, NB, ROWS, NT), np.float64)
    for half in range(2):
        for band in range(NB):
            for i in range(HF):
                k = band * FB + half * HF + i + 1
                angle = 2.0 * math.pi * ((time * k) % NT) / NT
                table[half, band, 2 * i] = np.cos(angle) / math.sqrt(NT)
                table[half, band, 2 * i + 1] = -np.sin(angle) / math.sqrt(NT)
    table = np.roll(table.reshape(2 * NB, ROWS, NT), 8, axis=0)
    return table.reshape(2 * NB * ROWS, NT).astype(np.float32).astype(jnp.bfloat16)


def tile_of(chip, half):
    return (chip // 4) * 8 + half * 4 + chip % 4


def shift_of(z):
    return (z * 4) % 16


def handler_chip(n, z):
    n0 = (n + 16 - shift_of(z)) % 16
    x = n0 % 4
    y = (n0 // 4 + x) % 4
    return x * 4 + y


def handler_number(chip, z):
    x = chip // 4
    y = chip % 4
    return (4 * ((y + 4 - x) % 4) + x + shift_of(z)) % 16


def onehot_groups(chunks, key_row, lo_row, l_ref, r_ref):
    low = lax.broadcasted_iota(jnp.int32, (CH, CH), 0).astype(F32).astype(BF16)
    zero = jnp.zeros((ROWS, CH), BF16)
    for n, chunk in enumerate(chunks):
        wide = chunk.astype(F32)
        key = jnp.broadcast_to(wide[key_row : key_row + 1], (ROWS, CH)).astype(BF16)
        lo = jnp.broadcast_to(wide[lo_row : lo_row + 1], (ROWS, CH)).astype(BF16)
        cols = slice(n * CH, (n + 1) * CH)
        for k in range(32):
            l_ref[k * ROWS : (k + 1) * ROWS, cols] = jnp.where(key == BF16(k), chunk, zero)
        lo_all = jnp.concatenate([lo] * (CH // ROWS), axis=0)
        r_ref[:, cols] = jnp.where(low == lo_all, BF16(1), BF16(0))


def onehot_cells(chunks, l_ref, r_ref):
    low = lax.broadcasted_iota(jnp.int32, (CH, CH), 0).astype(F32).astype(BF16)
    keys = lax.broadcasted_iota(jnp.int32, (32, CH), 0).astype(F32).astype(BF16)
    zero = jnp.zeros((32, CH), BF16)
    for n, chunk in enumerate(chunks):
        wide = chunk.astype(F32)

        def spread(row, rows):
            tile = jnp.broadcast_to(wide[row : row + 1], (ROWS, CH)).astype(BF16)
            return jnp.concatenate([tile] * (rows // ROWS), axis=0)

        cols = slice(n * CH, (n + 1) * CH)
        mask = spread(13, 32) == keys
        for v in range(11):
            l_ref[v * 32 : (v + 1) * 32, cols] = jnp.where(mask, spread(v, 32), zero)
        r_ref[:, cols] = jnp.where(low == spread(14, CH), BF16(1), BF16(0))


def nt_dot(left, right):
    return lax.dot_general(left, right, (((1,), (1,)), ((), ())), preferred_element_type=F32)


def kernel(
    raw_hbm, tw_hbm, own_hbm, off_hbm, out_ref,
    raw_ref, tw_ref, own_ref, off_ref,
    send1, rc1, l_ref, r_ref, acc_ref, send2, rc2, g_ref, rc3, s1, s2, mout,
    sem_in, sem1s, sem1r, sem2s, sem2r, sem3s, sem3r, sem4s, sem4r,
):
    band = lax.axis_index("band")
    tile = lax.axis_index("tile")
    x = tile // 8
    half = (tile // 4) % 2
    y = tile % 4
    chip = x * 4 + y
    zlo = band // 2
    core = band % 2
    z = half * 8 + zlo
    me1 = half * NB + band
    part = ((z + 12) % 16) // 8
    home = ((z + 12) % 8) * 2 + core

    def at_column(d):
        return {"band": d % NB, "tile": x * 8 + (d // NB) * 4 + y}

    def at_plane(c):
        return {"band": band, "tile": tile_of(c, half)}

    def at_level(c, level):
        return {"band": (level % 8) * 2 + core, "tile": tile_of(c, level // 8)}

    def column(r):
        return ((half + r // NB) % 2) * NB + (band + r) % NB

    barrier = pltpu.get_barrier_semaphore()

    def greet_column(r, carry):
        pl.semaphore_signal(barrier, inc=1, device_id=at_column(column(r)), device_id_type=MESH)
        return carry

    def greet_plane(r, carry):
        c = (chip + r) % 16
        pl.semaphore_signal(barrier, inc=1, device_id=at_plane(c), device_id_type=MESH)
        return carry

    loads = [
        pltpu.make_async_copy(src, dst, sem_in.at[n])
        for n, (src, dst) in enumerate(
            ((own_hbm, own_ref), (off_hbm, off_ref), (raw_hbm, raw_ref), (tw_hbm, tw_ref))
        )
    ]
    for load in loads:
        load.start()
    lax.fori_loop(1, 32, greet_column, 0)
    lax.fori_loop(1, 16, greet_plane, 0)

    loads[0].wait()
    loads[1].wait()
    ids = lax.broadcasted_iota(jnp.int32, (32, 128), 0)

    def owner_code(t):
        return (t // 8) * 8 + (t % 4) * 2 + (t // 4) % 2

    def count(i, carry):
        row = jnp.broadcast_to(owner_code(own_ref[pl.ds(i, 1), :]), (32, 128))
        before = jnp.where(i < 2 * band, 1.0, 0.0)
        return carry + jnp.where(row == ids, 1.0, 0.0) * before

    counts = lax.fori_loop(0, 32, count, jnp.zeros((32, 128), F32))
    counts = jnp.sum(counts, axis=1, keepdims=True)
    own = jnp.concatenate([own_ref[pl.ds(2 * band, 1), :], own_ref[pl.ds(2 * band + 1, 1), :]], axis=1)
    off = jnp.concatenate([off_ref[pl.ds(2 * band, 1), :], off_ref[pl.ds(2 * band + 1, 1), :]], axis=1)
    own = owner_code(own)
    hits = jnp.broadcast_to(own, (32, CH)) == lax.broadcasted_iota(jnp.int32, (32, CH), 0)
    hits = jnp.where(hits, 1.0, 0.0)
    earlier = lax.broadcasted_iota(jnp.int32, (CH, CH), 0) < lax.broadcasted_iota(jnp.int32, (CH, CH), 1)
    earlier = jnp.where(earlier, 1.0, 0.0).astype(BF16)
    ahead = jnp.dot(hits.astype(BF16), earlier, preferred_element_type=F32)
    rank = jnp.sum(hits * (ahead + counts), axis=0, keepdims=True)
    place = off % NG
    key2 = (place // CH) * 16 + off // NG
    row_id = lax.broadcasted_iota(jnp.int32, (ROWS, CH), 0)
    labels = jnp.where(row_id == 10, 1.0, 0.0)
    for at, value in ((11, own.astype(F32)), (12, rank), (13, key2.astype(F32)), (14, (place % CH).astype(F32))):
        labels = labels + jnp.where(row_id == at, jnp.broadcast_to(value, (ROWS, CH)), 0.0)

    loads[2].wait()
    loads[3].wait()
    spectra = nt_dot(tw_ref[...], raw_ref[...]).reshape(2 * NB, ROWS, CH)
    send1[...] = (spectra + labels[None]).astype(BF16)

    pl.semaphore_wait(barrier, 31 + 15)

    def copy1(d):
        return pltpu.make_async_remote_copy(
            src_ref=send1.at[d], dst_ref=rc1.at[me1], send_sem=sem1s.at[d], recv_sem=sem1r.at[me1],
            device_id=at_column(d), device_id_type=MESH,
        )

    def start1(r, carry):
        k = r % 8
        turn = (((k + 1) // 2) * (1 - 2 * (k % 2)) + 8) % 8
        d = (((half + (r // 8) % 2) % 2) * 8 + (zlo + turn) % 8) * 2 + r // 16

        @pl.when(d != me1)
        def _():
            copy1(d).start()

        return carry

    own1 = pltpu.make_async_copy(send1.at[me1], rc1.at[me1], sem1r.at[me1])
    own1.start()
    lax.fori_loop(0, 32, start1, 0)

    def copy2(s, c):
        return pltpu.make_async_remote_copy(
            src_ref=send2.at[s, c], dst_ref=rc2.at[s, chip], send_sem=sem2s.at[s, c], recv_sem=sem2r.at[s, chip],
            device_id=at_plane(c), device_id_type=MESH,
        )

    for s in range(2):
        first = ((half + s) % 2) * NB

        def slot(g, carry):
            sources = []
            for n in range(2):
                k = (1 - s) * 7 + (2 * s - 1) * (g * 2 + n)
                k = (zlo + 12 + ((k + 1) // 2) * (1 - 2 * (k % 2))) % 8
                sources += [first + 2 * k, first + 2 * k + 1]
            for src in sources:
                pltpu.make_async_copy(rc1.at[src], rc1.at[src], sem1r.at[src]).wait()
            onehot_groups([rc1[src] for src in sources], 11, 12, l_ref, r_ref)
            acc_ref[0] += nt_dot(l_ref[...], r_ref[...])
            return carry

        def start2(r, carry):
            q = r % 4
            dx = (2 + 4 - r // 4 + (r // 8) * (7 - 2 * (r // 4))) % 4
            dy = (2 + 4 - q + (q // 2) * (7 - 2 * q)) % 4
            copy2(s, ((x + dx) % 4) * 4 + (y + dy) % 4).start()
            return carry

        acc_ref[0] = jnp.zeros((512, CH), F32)
        lax.fori_loop(0, 4, slot, 0)
        send2[s] = acc_ref[0].reshape(16, 2, ROWS, CH).astype(BF16)
        own2 = pltpu.make_async_copy(send2.at[s, chip], rc2.at[s, chip], sem2r.at[s, chip])
        own2.start()
        lax.fori_loop(0, 15, start2, 0)

    def copy3(i, h):
        rows = pl.ds(pl.multiple_of(16 * tile_of(chip, h), 16), 16)
        if i < 4:
            freq, level, c = i, z, handler_chip(core * 4 + i, z)
        else:
            level = (z + 4 + 8 * (i - 4)) % 16
            freq, c = 4, handler_chip(8 + core * 2 + i - 4, level)
        remote = pltpu.make_async_remote_copy(
            src_ref=g_ref.at[freq, :, h], dst_ref=rc3.at[:, rows], send_sem=sem3s.at[i, h], recv_sem=sem3r,
            device_id=at_level(c, level), device_id_type=MESH,
        )
        local = pltpu.make_async_copy(g_ref.at[freq, :, h], rc3.at[:, rows], sem3r)
        return (c == chip) & (level == z), remote, local

    acc_ref[...] = jnp.zeros_like(acc_ref)
    for s in range(2):
        def bin_group(g, carry):
            sources = [(chip + g * 4 + n) % 16 for n in range(4)]
            for src in sources:
                pltpu.make_async_copy(rc2.at[s, src], rc2.at[s, src], sem2r.at[s, src]).wait()
            for h in range(2):
                onehot_cells([rc2[s, src, h] for src in sources], l_ref, r_ref)
                acc_ref[h, :352] += nt_dot(l_ref[:352], r_ref[...])
            return carry

        lax.fori_loop(0, 4, bin_group, 0)

    for h in range(2):
        for hi in range(2):
            many = acc_ref[h, 320 + hi * 16 : 336 + hi * 16, :]
            share = 1.0 / jnp.maximum(many, 1.0)
            for v in range(2 * HF):
                mean = acc_ref[h, v * 32 + hi * 16 : v * 32 + hi * 16 + 16, :] * share
                g_ref[v // 2, v % 2, h, :, hi * CH : (hi + 1) * CH] = mean.astype(BF16)
        for i in (4, 5, 0, 1, 2, 3):
            here, remote, local = copy3(i, h)
            if i >= 4:
                remote.start()
                continue

            @pl.when(jnp.logical_not(here))
            def _():
                remote.start()

            @pl.when(here)
            def _():
                local.start()

    number = handler_number(chip, z)
    far = number - core * 4
    near = number - 8 - core * 2
    is_far = (far >= 0) & (far < 4)
    is_near = (near >= 0) & (near < 2)
    far_place = part * HF + far
    near_place = ((half + 1 + near) % 2) * HF + 4

    def product(real, imag):
        m_real = jnp.dot(jnp.concatenate([real, -imag], axis=1), s1[...], preferred_element_type=F32)
        m_imag = jnp.dot(jnp.concatenate([real, imag], axis=1), s2[...], preferred_element_type=F32)
        scale = 1.0 / math.sqrt(NG)
        return [(m * scale).astype(BF16).reshape(16, 16, NG) for m in (m_real, m_imag)]

    def copy4(t):
        return pltpu.make_async_remote_copy(
            src_ref=mout.at[t], dst_ref=out_ref.at[far_place], send_sem=sem4s.at[t], recv_sem=sem4r,
            device_id={"band": home, "tile": t}, device_id_type=MESH,
        )

    def copy5(c):
        return pltpu.make_async_remote_copy(
            src_ref=mout.at[c], dst_ref=out_ref.at[near_place], send_sem=sem4s.at[c], recv_sem=sem4r,
            device_id=at_plane(c), device_id_type=MESH,
        )

    own5 = pltpu.make_async_copy(mout.at[chip], out_ref.at[near_place], sem4r)

    @pl.when(is_far | is_near)
    def _():
        pltpu.make_async_copy(rc3, rc3, sem3r).wait()
        for p in range(2):
            wide = rc3[p].astype(F32)
            sym = (0.5 * (wide + wide.T)).astype(BF16)
            s1[p * NG : (p + 1) * NG, :] = sym
            s2[(1 - p) * NG : (2 - p) * NG, :] = sym

    @pl.when(is_far)
    def _():
        def rows(turn, carry):
            b = (x // 2 + 1 + turn) % 2
            at = pl.ds(pl.multiple_of(b * 256, 256), 256)
            at_imag = pl.ds(pl.multiple_of(NG + b * 256, 256), 256)
            for p, m in enumerate(product(s1[at, :], s1[at_imag, :])):
                mout[pl.ds(b * 16, 16), p] = m

            def send(u, carry):
                q = u // 4
                up = (y + 2 + 4 - q + (q // 2) * (7 - 2 * q)) % 4
                along = 2 * b + (x + 1 + (u // 2) % 2) % 2
                copy4(tile_of(along * 4 + up, u % 2)).start()
                return carry

            return lax.fori_loop(0, 16, send, carry)

        lax.fori_loop(0, 2, rows, 0)

        def sent(t, carry):
            copy4(t).wait_send()
            return carry

        lax.fori_loop(0, 32, sent, 0)

    @pl.when(is_near)
    def _():
        real = [s1[pl.ds(pl.multiple_of(128 * n + 64 * half, 64), 64), :] for n in range(4)]
        imag = [s1[pl.ds(pl.multiple_of(NG + 128 * n + 64 * half, 64), 64), :] for n in range(4)]
        for p, m in enumerate(product(jnp.concatenate(real, axis=0), jnp.concatenate(imag, axis=0))):
            mout[:16, p] = m
        own5.start()

        def send(r, carry):
            copy5((chip + r) % 16).start()
            return carry

        def sent(r, carry):
            copy5((chip + r) % 16).wait_send()
            return carry

        lax.fori_loop(1, 16, send, 0)
        lax.fori_loop(1, 16, sent, 0)

    def sent1(r, carry):
        copy1(column(r)).wait_send()
        return carry

    def sent2(r, carry):
        copy2(0, (chip + r) % 16).wait_send()
        copy2(1, (chip + r) % 16).wait_send()
        return carry

    lax.fori_loop(1, 32, sent1, 0)
    lax.fori_loop(1, 16, sent2, 0)
    for i in range(6):
        for h in range(2):
            here, remote, local = copy3(i, h)
            if i >= 4:
                remote.wait_send()
                continue

            @pl.when(jnp.logical_not(here))
            def _():
                remote.wait_send()

    pltpu.make_async_copy(out_ref, out_ref, sem4r).wait()


def per_device(raw_traces, bin_owner, bin_offset, twiddle):
    vmem = pl.BlockSpec(memory_space=pltpu.VMEM)
    anywhere = pl.BlockSpec(memory_space=pltpu.HBM)
    strips = pl.pallas_call(
        kernel,
        out_shape=jax.ShapeDtypeStruct((FB, 2, 16, NG), BF16),
        in_specs=[anywhere] * 4,
        out_specs=vmem,
        scratch_shapes=[
            pltpu.VMEM((CH, NT), BF16),
            pltpu.VMEM((2 * NB * ROWS, NT), BF16),
            pltpu.VMEM((32, 128), jnp.int32),
            pltpu.VMEM((32, 128), jnp.int32),
            pltpu.VMEM((32, ROWS, CH), BF16),
            pltpu.VMEM((32, ROWS, CH), BF16),
            pltpu.VMEM((512, 4 * CH), BF16),
            pltpu.VMEM((CH, 4 * CH), BF16),
            pltpu.VMEM((2, 512, CH), F32),
            pltpu.VMEM((2, 16, 2, ROWS, CH), BF16),
            pltpu.VMEM((2, 16, 2, ROWS, CH), BF16),
            pltpu.VMEM((HF, 2, 2, 16, NG), BF16),
            pltpu.VMEM((2, NG, NG), BF16),
            pltpu.VMEM((2 * NG, NG), BF16),
            pltpu.VMEM((2 * NG, NG), BF16),
            pltpu.VMEM((NTILE, 2, 16, NG), BF16),
            pltpu.SemaphoreType.DMA((4,)),
            pltpu.SemaphoreType.DMA((32,)),
            pltpu.SemaphoreType.DMA((32,)),
            pltpu.SemaphoreType.DMA((2, 16)),
            pltpu.SemaphoreType.DMA((2, 16)),
            pltpu.SemaphoreType.DMA((6, 2)),
            pltpu.SemaphoreType.DMA,
            pltpu.SemaphoreType.DMA((32,)),
            pltpu.SemaphoreType.DMA,
        ],
        compiler_params=pltpu.CompilerParams(
            collective_id=0, has_side_effects=True, vmem_limit_bytes=60 * 1024 * 1024
        ),
    )(
        raw_traces.reshape(CH, NT),
        twiddle,
        bin_owner.reshape(32, 128),
        bin_offset.reshape(32, 128),
    )
    return strips.astype(F32)


def solution(mesh):
    table = twiddle_rows()
    step = jax.shard_map(
        per_device,
        mesh=mesh,
        in_specs=(P("tile", "band", None), P("tile", None, None), P("tile", None), P(None, None)),
        out_specs=P("band", None, "tile", None),
        check_vma=False,
    )
    return lambda raw_traces, bin_owner, bin_offset: step(raw_traces, bin_owner, bin_offset, jnp.asarray(table))
```

```python
import math

import jax
import jax.numpy as jnp
import numpy as np
from jax import lax
from jax.experimental import pallas as pl
from jax.experimental.pallas import tpu as pltpu
from jax.sharding import PartitionSpec as P

NG = 512
NT = 2048
FB = 10
NB = 16
NTILE = 32
HF = 5
ROWS = 16
CH = 256
MESH = pl.DeviceIdType.MESH
F32 = jnp.float32
BF16 = jnp.bfloat16


def twiddle_rows():
    time = np.arange(NT, dtype=np.int64)
    table = np.zeros((2, NB, ROWS, NT), np.float64)
    for half in range(2):
        for band in range(NB):
            for i in range(HF):
                k = band * FB + half * HF + i + 1
                angle = 2.0 * math.pi * ((time * k) % NT) / NT
                table[half, band, 2 * i] = np.cos(angle) / math.sqrt(NT)
                table[half, band, 2 * i + 1] = -np.sin(angle) / math.sqrt(NT)
    table = np.roll(table.reshape(2 * NB, ROWS, NT), 8, axis=0)
    return table.reshape(2 * NB * ROWS, NT).astype(np.float32).astype(jnp.bfloat16)


def tile_of(chip, half):
    return (chip // 4) * 8 + half * 4 + chip % 4


def shift_of(z):
    return (z * 4) % 16


def handler_chip(n, z):
    n0 = (n + 16 - shift_of(z)) % 16
    x = n0 % 4
    y = (n0 // 4 + x) % 4
    return x * 4 + y


def handler_number(chip, z):
    x = chip // 4
    y = chip % 4
    return (4 * ((y + 4 - x) % 4) + x + shift_of(z)) % 16


def onehot_groups(chunks, key_row, lo_row, l_ref, r_ref):
    low = lax.broadcasted_iota(jnp.int32, (CH, CH), 0).astype(F32).astype(BF16)
    zero = jnp.zeros((ROWS, CH), BF16)
    for n, chunk in enumerate(chunks):
        wide = chunk.astype(F32)
        key = jnp.broadcast_to(wide[key_row : key_row + 1], (ROWS, CH)).astype(BF16)
        lo = jnp.broadcast_to(wide[lo_row : lo_row + 1], (ROWS, CH)).astype(BF16)
        cols = slice(n * CH, (n + 1) * CH)
        for k in range(32):
            l_ref[k * ROWS : (k + 1) * ROWS, cols] = jnp.where(key == BF16(k), chunk, zero)
        lo_all = jnp.concatenate([lo] * (CH // ROWS), axis=0)
        r_ref[:, cols] = jnp.where(low == lo_all, BF16(1), BF16(0))


def onehot_cells(chunks, l_ref, r_ref):
    low = lax.broadcasted_iota(jnp.int32, (CH, CH), 0).astype(F32).astype(BF16)
    keys = lax.broadcasted_iota(jnp.int32, (32, CH), 0).astype(F32).astype(BF16)
    zero = jnp.zeros((32, CH), BF16)
    for n, chunk in enumerate(chunks):
        wide = chunk.astype(F32)

        def spread(row, rows):
            tile = jnp.broadcast_to(wide[row : row + 1], (ROWS, CH)).astype(BF16)
            return jnp.concatenate([tile] * (rows // ROWS), axis=0)

        cols = slice(n * CH, (n + 1) * CH)
        mask = spread(13, 32) == keys
        for v in range(11):
            l_ref[v * 32 : (v + 1) * 32, cols] = jnp.where(mask, spread(v, 32), zero)
        r_ref[:, cols] = jnp.where(low == spread(14, CH), BF16(1), BF16(0))


def nt_dot(left, right):
    return lax.dot_general(left, right, (((1,), (1,)), ((), ())), preferred_element_type=F32)


def kernel(
    raw_hbm, tw_hbm, own_hbm, off_hbm, out_ref,
    raw_ref, tw_ref, own_ref, off_ref,
    send1, rc1, l_ref, r_ref, acc_ref, send2, rc2, g_ref, rc3, s1, s2, mout,
    sem_in, sem1s, sem1r, sem2s, sem2r, sem3s, sem3r, sem4s, sem4r,
):
    band = lax.axis_index("band")
    tile = lax.axis_index("tile")
    x = tile // 8
    half = (tile // 4) % 2
    y = tile % 4
    chip = x * 4 + y
    zlo = band // 2
    core = band % 2
    z = half * 8 + zlo
    me1 = half * NB + band
    part = ((z + 12) % 16) // 8
    home = ((z + 12) % 8) * 2 + core

    def at_column(d):
        return {"band": d % NB, "tile": x * 8 + (d // NB) * 4 + y}

    def at_plane(c):
        return {"band": band, "tile": tile_of(c, half)}

    def at_level(c, level):
        return {"band": (level % 8) * 2 + core, "tile": tile_of(c, level // 8)}

    def column(r):
        return ((half + r // NB) % 2) * NB + (band + r) % NB

    barrier = pltpu.get_barrier_semaphore()

    def greet_column(r, carry):
        pl.semaphore_signal(barrier, inc=1, device_id=at_column(column(r)), device_id_type=MESH)
        return carry

    def greet_plane(r, carry):
        c = (chip + r) % 16
        pl.semaphore_signal(barrier, inc=1, device_id=at_plane(c), device_id_type=MESH)
        return carry

    loads = [
        pltpu.make_async_copy(src, dst, sem_in.at[n])
        for n, (src, dst) in enumerate(
            ((own_hbm, own_ref), (off_hbm, off_ref), (raw_hbm, raw_ref), (tw_hbm, tw_ref))
        )
    ]
    for load in loads:
        load.start()
    lax.fori_loop(1, 32, greet_column, 0)
    lax.fori_loop(1, 16, greet_plane, 0)

    loads[0].wait()
    loads[1].wait()
    ids = lax.broadcasted_iota(jnp.int32, (32, 128), 0)

    def owner_code(t):
        return (t // 8) * 8 + (t % 4) * 2 + (t // 4) % 2

    def count(i, carry):
        row = jnp.broadcast_to(owner_code(own_ref[pl.ds(i, 1), :]), (32, 128))
        before = jnp.where(i < 2 * band, 1.0, 0.0)
        return carry + jnp.where(row == ids, 1.0, 0.0) * before

    counts = lax.fori_loop(0, 32, count, jnp.zeros((32, 128), F32))
    counts = jnp.sum(counts, axis=1, keepdims=True)
    own = jnp.concatenate([own_ref[pl.ds(2 * band, 1), :], own_ref[pl.ds(2 * band + 1, 1), :]], axis=1)
    off = jnp.concatenate([off_ref[pl.ds(2 * band, 1), :], off_ref[pl.ds(2 * band + 1, 1), :]], axis=1)
    own = owner_code(own)
    hits = jnp.broadcast_to(own, (32, CH)) == lax.broadcasted_iota(jnp.int32, (32, CH), 0)
    hits = jnp.where(hits, 1.0, 0.0)
    earlier = lax.broadcasted_iota(jnp.int32, (CH, CH), 0) < lax.broadcasted_iota(jnp.int32, (CH, CH), 1)
    earlier = jnp.where(earlier, 1.0, 0.0).astype(BF16)
    ahead = jnp.dot(hits.astype(BF16), earlier, preferred_element_type=F32)
    rank = jnp.sum(hits * (ahead + counts), axis=0, keepdims=True)
    place = off % NG
    key2 = (place // CH) * 16 + off // NG
    row_id = lax.broadcasted_iota(jnp.int32, (ROWS, CH), 0)
    labels = jnp.where(row_id == 10, 1.0, 0.0)
    for at, value in ((11, own.astype(F32)), (12, rank), (13, key2.astype(F32)), (14, (place % CH).astype(F32))):
        labels = labels + jnp.where(row_id == at, jnp.broadcast_to(value, (ROWS, CH)), 0.0)

    loads[2].wait()
    loads[3].wait()
    spectra = nt_dot(tw_ref[...], raw_ref[...]).reshape(2 * NB, ROWS, CH)
    send1[...] = (spectra + labels[None]).astype(BF16)

    pl.semaphore_wait(barrier, 31 + 15)

    def copy1(d):
        return pltpu.make_async_remote_copy(
            src_ref=send1.at[d], dst_ref=rc1.at[me1], send_sem=sem1s.at[d], recv_sem=sem1r.at[me1],
            device_id=at_column(d), device_id_type=MESH,
        )

    def start1(r, carry):
        k = r % 8
        turn = (((k + 1) // 2) * (1 - 2 * (k % 2)) + 8) % 8
        d = (((half + (r // 8) % 2) % 2) * 8 + (zlo + turn) % 8) * 2 + r // 16

        @pl.when(d != me1)
        def _():
            copy1(d).start()

        return carry

    own1 = pltpu.make_async_copy(send1.at[me1], rc1.at[me1], sem1r.at[me1])
    own1.start()
    lax.fori_loop(0, 32, start1, 0)

    def copy2(s, c):
        return pltpu.make_async_remote_copy(
            src_ref=send2.at[s, c], dst_ref=rc2.at[s, chip], send_sem=sem2s.at[s, c], recv_sem=sem2r.at[s, chip],
            device_id=at_plane(c), device_id_type=MESH,
        )

    for s in range(2):
        first = ((half + s) % 2) * NB

        def slot(g, carry):
            sources = []
            for n in range(2):
                k = (1 - s) * 7 + (2 * s - 1) * (g * 2 + n)
                k = (zlo + 12 + ((k + 1) // 2) * (1 - 2 * (k % 2))) % 8
                sources += [first + 2 * k, first + 2 * k + 1]
            for src in sources:
                pltpu.make_async_copy(rc1.at[src], rc1.at[src], sem1r.at[src]).wait()
            onehot_groups([rc1[src] for src in sources], 11, 12, l_ref.at[0], r_ref.at[0])
            acc_ref[0] += nt_dot(l_ref[0], r_ref[0])
            return carry

        def start2(r, carry):
            q = r % 4
            dx = (2 + 4 - r // 4 + (r // 8) * (7 - 2 * (r // 4))) % 4
            dy = (2 + 4 - q + (q // 2) * (7 - 2 * q)) % 4
            copy2(s, ((x + dx) % 4) * 4 + (y + dy) % 4).start()
            return carry

        acc_ref[0] = jnp.zeros((512, CH), F32)
        lax.fori_loop(0, 4, slot, 0)
        send2[s] = acc_ref[0].reshape(16, 2, ROWS, CH).astype(BF16)
        own2 = pltpu.make_async_copy(send2.at[s, chip], rc2.at[s, chip], sem2r.at[s, chip])
        own2.start()
        lax.fori_loop(0, 15, start2, 0)

    def copy3(i, h):
        rows = pl.ds(pl.multiple_of(16 * tile_of(chip, h), 16), 16)
        if i < 4:
            freq, level, c = i, z, handler_chip(core * 4 + i, z)
        else:
            level = (z + 4 + 8 * (i - 4)) % 16
            freq, c = 4, handler_chip(8 + core * 2 + i - 4, level)
        remote = pltpu.make_async_remote_copy(
            src_ref=g_ref.at[freq, :, h], dst_ref=rc3.at[:, rows], send_sem=sem3s.at[i, h], recv_sem=sem3r,
            device_id=at_level(c, level), device_id_type=MESH,
        )
        local = pltpu.make_async_copy(g_ref.at[freq, :, h], rc3.at[:, rows], sem3r)
        return (c == chip) & (level == z), remote, local

    acc_ref[...] = jnp.zeros_like(acc_ref)
    for s in range(2):
        def bin_group(g, carry):
            sources = [(chip + g * 4 + n) % 16 for n in range(4)]
            for src in sources:
                pltpu.make_async_copy(rc2.at[s, src], rc2.at[s, src], sem2r.at[s, src]).wait()
            for h in range(2):
                onehot_cells([rc2[s, src, h] for src in sources], l_ref.at[h], r_ref.at[h])
                acc_ref[h, :352] += nt_dot(l_ref[h, :352], r_ref[h])
            return carry

        lax.fori_loop(0, 4, bin_group, 0)

    for h in range(2):
        for hi in range(2):
            many = acc_ref[h, 320 + hi * 16 : 336 + hi * 16, :]
            share = 1.0 / jnp.maximum(many, 1.0)
            for v in range(2 * HF):
                mean = acc_ref[h, v * 32 + hi * 16 : v * 32 + hi * 16 + 16, :] * share
                g_ref[v // 2, v % 2, h, :, hi * CH : (hi + 1) * CH] = mean.astype(BF16)
        for i in (4, 5, 0, 1, 2, 3):
            here, remote, local = copy3(i, h)
            if i >= 4:
                remote.start()
                continue

            @pl.when(jnp.logical_not(here))
            def _():
                remote.start()

            @pl.when(here)
            def _():
                local.start()

    number = handler_number(chip, z)
    far = number - core * 4
    near = number - 8 - core * 2
    is_far = (far >= 0) & (far < 4)
    is_near = (near >= 0) & (near < 2)
    far_place = part * HF + far
    near_place = ((half + 1 + near) % 2) * HF + 4

    def product(real, imag):
        m_real = jnp.dot(jnp.concatenate([real, -imag], axis=1), s1[...], preferred_element_type=F32)
        m_imag = jnp.dot(jnp.concatenate([real, imag], axis=1), s2[...], preferred_element_type=F32)
        scale = 1.0 / math.sqrt(NG)
        return [(m * scale).astype(BF16).reshape(16, 16, NG) for m in (m_real, m_imag)]

    def copy4(t):
        return pltpu.make_async_remote_copy(
            src_ref=mout.at[t], dst_ref=out_ref.at[far_place], send_sem=sem4s.at[t], recv_sem=sem4r,
            device_id={"band": home, "tile": t}, device_id_type=MESH,
        )

    def copy5(c):
        return pltpu.make_async_remote_copy(
            src_ref=mout.at[c], dst_ref=out_ref.at[near_place], send_sem=sem4s.at[c], recv_sem=sem4r,
            device_id=at_plane(c), device_id_type=MESH,
        )

    own5 = pltpu.make_async_copy(mout.at[chip], out_ref.at[near_place], sem4r)

    @pl.when(is_far | is_near)
    def _():
        pltpu.make_async_copy(rc3, rc3, sem3r).wait()
        for p in range(2):
            wide = rc3[p].astype(F32)
            sym = (0.5 * (wide + wide.T)).astype(BF16)
            s1[p * NG : (p + 1) * NG, :] = sym
            s2[(1 - p) * NG : (2 - p) * NG, :] = sym

    @pl.when(is_far)
    def _():
        def rows(turn, carry):
            b = (x // 2 + 1 + turn) % 2
            at = pl.ds(pl.multiple_of(b * 256, 256), 256)
            at_imag = pl.ds(pl.multiple_of(NG + b * 256, 256), 256)
            for p, m in enumerate(product(s1[at, :], s1[at_imag, :])):
                mout[pl.ds(b * 16, 16), p] = m

            def send(u, carry):
                q = u // 4
                up = (y + 2 + 4 - q + (q // 2) * (7 - 2 * q)) % 4
                along = 2 * b + (x + 1 + (u // 2) % 2) % 2
                copy4(tile_of(along * 4 + up, u % 2)).start()
                return carry

            return lax.fori_loop(0, 16, send, carry)

        lax.fori_loop(0, 2, rows, 0)

        def sent(t, carry):
            copy4(t).wait_send()
            return carry

        lax.fori_loop(0, 32, sent, 0)

    @pl.when(is_near)
    def _():
        real = [s1[pl.ds(pl.multiple_of(128 * n + 64 * half, 64), 64), :] for n in range(4)]
        imag = [s1[pl.ds(pl.multiple_of(NG + 128 * n + 64 * half, 64), 64), :] for n in range(4)]
        for p, m in enumerate(product(jnp.concatenate(real, axis=0), jnp.concatenate(imag, axis=0))):
            mout[:16, p] = m
        own5.start()

        def send(r, carry):
            copy5((chip + r) % 16).start()
            return carry

        def sent(r, carry):
            copy5((chip + r) % 16).wait_send()
            return carry

        lax.fori_loop(1, 16, send, 0)
        lax.fori_loop(1, 16, sent, 0)

    def sent1(r, carry):
        copy1(column(r)).wait_send()
        return carry

    def sent2(r, carry):
        copy2(0, (chip + r) % 16).wait_send()
        copy2(1, (chip + r) % 16).wait_send()
        return carry

    lax.fori_loop(1, 32, sent1, 0)
    lax.fori_loop(1, 16, sent2, 0)
    for i in range(6):
        for h in range(2):
            here, remote, local = copy3(i, h)
            if i >= 4:
                remote.wait_send()
                continue

            @pl.when(jnp.logical_not(here))
            def _():
                remote.wait_send()

    pltpu.make_async_copy(out_ref, out_ref, sem4r).wait()


def per_device(raw_traces, bin_owner, bin_offset, twiddle):
    vmem = pl.BlockSpec(memory_space=pltpu.VMEM)
    anywhere = pl.BlockSpec(memory_space=pltpu.HBM)
    strips = pl.pallas_call(
        kernel,
        out_shape=jax.ShapeDtypeStruct((FB, 2, 16, NG), BF16),
        in_specs=[anywhere] * 4,
        out_specs=vmem,
        scratch_shapes=[
            pltpu.VMEM((CH, NT), BF16),
            pltpu.VMEM((2 * NB * ROWS, NT), BF16),
            pltpu.VMEM((32, 128), jnp.int32),
            pltpu.VMEM((32, 128), jnp.int32),
            pltpu.VMEM((32, ROWS, CH), BF16),
            pltpu.VMEM((32, ROWS, CH), BF16),
            pltpu.VMEM((2, 512, 4 * CH), BF16),
            pltpu.VMEM((2, CH, 4 * CH), BF16),
            pltpu.VMEM((2, 512, CH), F32),
            pltpu.VMEM((2, 16, 2, ROWS, CH), BF16),
            pltpu.VMEM((2, 16, 2, ROWS, CH), BF16),
            pltpu.VMEM((HF, 2, 2, 16, NG), BF16),
            pltpu.VMEM((2, NG, NG), BF16),
            pltpu.VMEM((2 * NG, NG), BF16),
            pltpu.VMEM((2 * NG, NG), BF16),
            pltpu.VMEM((NTILE, 2, 16, NG), BF16),
            pltpu.SemaphoreType.DMA((4,)),
            pltpu.SemaphoreType.DMA((32,)),
            pltpu.SemaphoreType.DMA((32,)),
            pltpu.SemaphoreType.DMA((2, 16)),
            pltpu.SemaphoreType.DMA((2, 16)),
            pltpu.SemaphoreType.DMA((6, 2)),
            pltpu.SemaphoreType.DMA,
            pltpu.SemaphoreType.DMA((32,)),
            pltpu.SemaphoreType.DMA,
        ],
        compiler_params=pltpu.CompilerParams(
            collective_id=0, has_side_effects=True, vmem_limit_bytes=60 * 1024 * 1024
        ),
    )(
        raw_traces.reshape(CH, NT),
        twiddle,
        bin_owner.reshape(32, 128),
        bin_offset.reshape(32, 128),
    )
    return strips.astype(F32)


def solution(mesh):
    table = twiddle_rows()
    step = jax.shard_map(
        per_device,
        mesh=mesh,
        in_specs=(P("tile", "band", None), P("tile", None, None), P("tile", None), P(None, None)),
        out_specs=P("band", None, "tile", None),
        check_vma=False,
    )
    return lambda raw_traces, bin_owner, bin_offset: step(raw_traces, bin_owner, bin_offset, jnp.asarray(table))
```
